32 devices in a mesh: group: 2 (over y), chan: 4 (over z), blk: 2 (over x), pol: 2 (over core).
Axes of the slice: x: 2, y: 2, z: 4, core: 2. Of those that a mesh axis runs over, the one named last changes fastest.
Arguments:
- voltages: bfloat16 [4096, 2, 32768], P(('group', 'chan', 'blk'), None, 'pol'), parts along dimension 0, may hold values from -6 to 6
- history: bfloat16 [4096, 2, 14336], P(('group', 'chan', 'blk')), parts along dimension 0, may hold values from -6 to 6
- block_pairs: int32 [4, 2], replicated, may hold values from 0 to 31, as said below
- owner_map: int32 [4], replicated, may hold values from 0 to 1, as said below
- weights: int32 [4], replicated, may hold values from 1 to 8
Outputs:
- visibilities: float32 [8, 6, 2, 128, 128], P(('group', 'chan'), 'blk', 'pol'), parts along dimension 0
The draws below stay inside these ranges and needn't reach their ends.
There are 2 independent parts, one for each index of `group`. The reference program is written for one: setup_inputs(seed, part) draws one part's arguments, and reference() takes and returns one part's arrays. A program takes and returns all parts, laid end to end along the dimension named above; an argument that names none is the same for every part. Nothing has to cross between parts.
Inputs may be any that keep to these rules, and one draw needn't show every extreme that they name: `block_pairs`: each row holds two antenna-block indices, the first not larger than the second; no two rows are equal. `owner_map`: no owner gets more than 3 blocks; one owner gets exactly 3; every other owner gets at most two.
All inputs are finite; a program needn't handle non-finite values.
Results may differ from the reference program's by a relative error of at most 0.0034.
Values may be sent and summed in bfloat16 or wider, within the bound.
A program may use at most 192 MiB of HBM per device.

```python
import math
import jax
import jax.numpy as jnp
import numpy as np
from jax import lax

A = 2048
FEEDS = 2
ABLK = 64
NF = 2048
TAPS = 8
CH = 1024
SPEC_ALL = 16
TIME = 32768
NABL = 32
NB = 4
OWNERS = 2
MOST = 3
SLOTS = 6
COARSE = 4
CHG = 256


def draw_block_pairs(key, part):
    key = jax.random.fold_in(key, 11)
    pick_key, pair_key = jax.random.split(key)
    subset = 2
    while subset < NABL and subset * (subset + 1) // 2 < 2 * NB:
        subset = subset + 1
    middle = (1 + jax.random.permutation(pick_key, NABL - 2)).astype(jnp.int32)
    chosen = jnp.concatenate([jnp.array([0, NABL - 1], jnp.int32), middle[:subset - 2]])
    upper_rows, upper_cols = np.triu_indices(subset)
    total_pairs = upper_rows.shape[0]
    order = jax.random.permutation(pair_key, total_pairs).astype(jnp.int32)
    order = jnp.where(order == 1, order[0], order)
    order = order.at[0].set(1)
    picked = order[:NB]
    first_block = chosen[jnp.asarray(upper_rows, jnp.int32)[picked]]
    second = chosen[jnp.asarray(upper_cols, jnp.int32)[picked]]
    return jnp.stack([jnp.minimum(first_block, second), jnp.maximum(first_block, second)], axis=1).astype(jnp.int32)


def draw_owner_map(key, part):
    key = jax.random.fold_in(key, 23)
    busy_key, order_key = jax.random.split(key)
    busy_owner = jax.random.randint(busy_key, (), 0, OWNERS).astype(jnp.int32)
    shuffled = jax.random.permutation(order_key, NB).astype(jnp.int32)
    position = jnp.arange(NB, dtype=jnp.int32)
    others = (busy_owner + 1 + (position - MOST) % (OWNERS - 1)) % OWNERS
    owner_value = jnp.where(position < MOST, busy_owner, others).astype(jnp.int32)
    return jnp.zeros((NB,), jnp.int32).at[shuffled].set(owner_value)


def with_ends(entries, rng, smallest, high):
    dims = entries.shape
    place = [jax.random.randint(jax.random.fold_in(rng, axis), (), 0, dims[axis]) for axis in range(len(dims))]
    entries = entries.at[tuple(place)].set(smallest)
    longest = dims.index(max(dims))
    place[longest] = (place[longest] + 1) % dims[longest]
    return entries.at[tuple(place)].set(high)


def shard_levels(key, dims, pieces, low, high):
    gain = 1.0
    for dim, blocks in pieces:
        draws = jax.random.uniform(jax.random.fold_in(jax.random.fold_in(key, 6), dim), (blocks,), jnp.float32, low / len(pieces), high / len(pieces))
        gain = gain * jnp.repeat(jnp.exp(draws), dims[dim] // blocks).reshape((-1,) + (1,) * (len(dims) - 1 - dim))
    return gain


def bell_draw(stream_key, extent, deviation, bound, pieces=(), kind=jnp.bfloat16):
    values = deviation * jax.random.normal(stream_key, extent, jnp.float32)
    if pieces:
        values = values * shard_levels(stream_key, extent, pieces, -0.22, 0.18)
    return jnp.clip(values, -bound, bound).astype(kind)


def setup_inputs(seed: int = 0, part: int = 0) -> dict:
    seeds = jax.random.split(jax.random.key(seed), 6)
    part_splits = jax.random.split(jax.random.fold_in(seeds[5], part), 6)
    return {
        "voltages": bell_draw(part_splits[0], (A, FEEDS, TIME), 1.0, 6.0, ((0, 8), (2, 2))),
        "history": bell_draw(part_splits[1], (A, FEEDS, (TAPS - 1) * NF), 1.0, 6.0, ((0, 8),)),
        "block_pairs": draw_block_pairs(jax.random.fold_in(seeds[5], 71), part),
        "owner_map": draw_owner_map(jax.random.fold_in(seeds[5], 71), part),
        "weights": with_ends(jax.random.randint(seeds[4], (NB,), 1, 9), jax.random.fold_in(seeds[4], 1), 1, 8).astype(jnp.int32),
    }


def prototype():
    length = TAPS * NF
    position = jnp.arange(length, dtype=jnp.float32)
    taper_win = 0.54 - 0.46 * jnp.cos(2.0 * math.pi / (length - 1) * position)
    raw_taps = jnp.sinc((position - length / 2) / NF) * taper_win
    return raw_taps / jnp.sqrt(jnp.sum(raw_taps * raw_taps) / NF)

def dft_table():
    sample = jnp.arange(NF, dtype=jnp.int32)[:, None]
    channel = jnp.arange(NF // 2, dtype=jnp.int32)[None, :]
    phases = (sample * channel % NF).astype(jnp.float32) * (2.0 * math.pi / NF)
    normalize = 1.0 / math.sqrt(NF)
    cosine = (jnp.cos(phases) * normalize).astype(jnp.bfloat16)
    sine_part = (jnp.sin(phases) * -normalize).astype(jnp.bfloat16)
    return (cosine, sine_part)

def reference(voltages, history, block_pairs, owner_map, weights):
    window = prototype().reshape(TAPS, NF)
    cosine, sine_part = dft_table()
    cos_wide = cosine.astype(jnp.float32)
    sin_wide = sine_part.astype(jnp.float32)
    block_rows = ABLK * FEEDS

    def channelize(block_index):
        start = block_index * ABLK
        fresh = lax.dynamic_slice_in_dim(voltages, start, ABLK, 0)
        older_part = lax.dynamic_slice_in_dim(history, start, ABLK, 0)
        signal = jnp.concatenate([older_part, fresh], axis=2).astype(jnp.float32)
        signal = signal.reshape(ABLK, FEEDS, TAPS - 1 + SPEC_ALL, NF)
        filtered = jnp.zeros((ABLK, FEEDS, SPEC_ALL, NF), jnp.float32)
        for tap_index in range(TAPS):
            filtered = filtered + window[tap_index] * signal[:, :, tap_index:tap_index + SPEC_ALL, :]
        narrow = lax.optimization_barrier(filtered.astype(jnp.bfloat16))
        flat_rows = narrow.astype(jnp.float32).reshape(block_rows * SPEC_ALL, NF)
        spectra_re = jnp.dot(flat_rows, cos_wide, precision=lax.Precision.HIGHEST).astype(jnp.bfloat16)
        spectra_im = jnp.dot(flat_rows, sin_wide, precision=lax.Precision.HIGHEST).astype(jnp.bfloat16)
        return (spectra_re.reshape(block_rows, SPEC_ALL, CH), spectra_im.reshape(block_rows, SPEC_ALL, CH))
    spectra_re, spectra_im = lax.map(channelize, jnp.arange(NABL, dtype=jnp.int32))
    spectra_re = spectra_re.reshape(NABL, block_rows, SPEC_ALL, COARSE, CHG)
    spectra_im = spectra_im.reshape(NABL, block_rows, SPEC_ALL, COARSE, CHG)

    def contract(first_part, second_part):
        return jnp.einsum('rsgc,qsgc->grq', first_part, second_part, precision=lax.Precision.HIGHEST)

    def correlate(pair_row):
        left_re = spectra_re[pair_row[0]].astype(jnp.float32)
        left_im = spectra_im[pair_row[0]].astype(jnp.float32)
        right_re = spectra_re[pair_row[1]].astype(jnp.float32)
        right_im = spectra_im[pair_row[1]].astype(jnp.float32)
        acc_re = contract(left_re, right_re) + contract(left_im, right_im)
        acc_im = contract(left_im, right_re) - contract(left_re, right_im)
        return jnp.stack([acc_re, acc_im], axis=1)
    products = lax.map(correlate, block_pairs)
    factor = weights.astype(jnp.float32) / math.sqrt(CHG * SPEC_ALL)
    scaled = products * factor[:, None, None, None, None]
    ordinal = jnp.arange(NB, dtype=jnp.int32)
    same_owner = owner_map[None, :] == owner_map[:, None]
    earlier = ordinal[None, :] < ordinal[:, None]
    ranking = lax.optimization_barrier(jnp.sum(jnp.logical_and(same_owner, earlier), axis=1)).astype(jnp.int32)
    slot_index = owner_map * MOST + ranking
    result = jnp.zeros((COARSE, SLOTS, 2, block_rows, block_rows), jnp.float32)
    return result.at[:, slot_index].set(jnp.transpose(scaled, (1, 0, 2, 3, 4)))
```

```python
import math
from functools import partial

import jax
import jax.numpy as jnp
import numpy as np
from jax import lax
from jax.sharding import PartitionSpec as P

ABLK = 64
NF = 2048
TAPS = 8
CAP = 4


def from_behind(block, axis, distance):
    devices = range(lax.axis_size(axis))
    route = [(i - distance, i) for i in devices if i - distance in devices]
    return lax.ppermute(block, axis, route)


def prototype():
    length = TAPS * NF
    position = jnp.arange(length, dtype=jnp.float32)
    taper_win = 0.54 - 0.46 * jnp.cos(2.0 * math.pi / (length - 1) * position)
    raw_taps = jnp.sinc((position - length / 2) / NF) * taper_win
    return raw_taps / jnp.sqrt(jnp.sum(raw_taps * raw_taps) / NF)


def dft_rows():
    sample = jnp.arange(NF, dtype=jnp.int32)[:, None]
    channel = jnp.arange(NF // 2, dtype=jnp.int32)[None, :]
    phases = (sample * channel % NF).astype(jnp.float32) * (2.0 * math.pi / NF)
    normalize = 1.0 / math.sqrt(NF)
    cosine = (jnp.cos(phases) * normalize).astype(jnp.bfloat16)
    sine_part = (jnp.sin(phases) * -normalize).astype(jnp.bfloat16)
    return jnp.stack([cosine, sine_part], axis=1)


def slot_sources(owner_map, owners, capacity):
    blocks = owner_map.shape[0]
    ordinal = jnp.arange(blocks, dtype=jnp.int32)
    same_owner = owner_map[None, :] == owner_map[:, None]
    earlier = ordinal[None, :] < ordinal[:, None]
    ranking = jnp.sum(jnp.logical_and(same_owner, earlier), axis=1)
    position = jnp.arange(capacity, dtype=jnp.int32)
    matched = jnp.logical_and(
        owner_map[None, None, :] == owners[:, None, None],
        ranking[None, None, :] == position[None, :, None],
    )
    source = jnp.sum(jnp.where(matched, ordinal[None, None, :], 0), axis=2)
    filled = jnp.any(matched, axis=2)
    return (matched, source, filled)


def constants(pieces):
    length = TAPS * NF
    position = np.arange(length, dtype=np.float64)
    taper_win = 0.54 - 0.46 * np.cos(2.0 * math.pi / (length - 1) * position)
    raw_taps = np.sinc((position - length / 2) / NF) * taper_win
    window = raw_taps / np.sqrt(np.sum(raw_taps * raw_taps) / NF)
    sample = np.arange(NF, dtype=np.int64)[:, None]
    channel = np.arange(NF // 2, dtype=np.int64)[None, :]
    phases = (sample * channel % NF).astype(np.float32) * np.float32(2.0 * math.pi / NF)
    phases = phases.astype(np.float64)
    normalize = np.float32(1.0 / math.sqrt(NF))
    cosine = np.cos(phases).astype(np.float32) * normalize
    sine = np.sin(phases).astype(np.float32) * -normalize
    table = np.stack([cosine, sine], axis=1).reshape(NF, 2, pieces, -1)
    table = table.transpose(0, 2, 1, 3).reshape(NF, -1)
    return window.astype(np.float32).reshape(TAPS, NF), table.astype(jnp.bfloat16)


def listed_blocks(block_pairs, homes, held):
    listed = jnp.any(
        block_pairs.reshape(-1)[:, None] == jnp.arange(homes * held, dtype=jnp.int32)[None, :],
        axis=0,
    ).reshape(homes, held)
    rank = jnp.cumsum(listed.astype(jnp.int32), axis=1) - 1
    most = jnp.max(rank[:, -1]) + 1
    return listed, rank, most


def compact(count, voltages, history, block_pairs, owner_map, weights):
    antennas, feed_count, samples = voltages.shape
    spectra_dev = samples // NF
    rows = ABLK * feed_count
    n_chan, n_blk, n_pol = (lax.axis_size(a) for a in ("chan", "blk", "pol"))
    homes = n_chan * n_blk
    held = antennas // ABLK
    me = lax.axis_index("chan") * n_blk + lax.axis_index("blk")
    listed, rank, _ = listed_blocks(block_pairs, homes, held)
    mine = lax.dynamic_index_in_dim(jnp.where(listed, rank, -1), me, 0, keepdims=False)
    window, table = constants(homes)
    per_dev = NF // homes
    spectra = []
    for k in range(count):
        local = jnp.sum(jnp.where(mine == k, jnp.arange(held, dtype=jnp.int32), 0))
        fresh = lax.dynamic_slice_in_dim(voltages, local * ABLK, ABLK, 0).reshape(rows, samples)
        older = lax.dynamic_slice_in_dim(history, local * ABLK, ABLK, 0)
        older = older.reshape(rows, (TAPS - 1) * NF)
        carried = from_behind(fresh[:, samples - (TAPS - 1) * NF :], "pol", 1)
        older = jnp.where(lax.axis_index("pol") == 0, older, carried)
        frames = [older[:, i * NF : (i + 1) * NF] for i in range(TAPS - 1)]
        frames += [fresh[:, i * NF : (i + 1) * NF] for i in range(spectra_dev)]
        filtered = []
        for s in range(spectra_dev):
            total = jnp.zeros((rows, NF), jnp.float32)
            for tap in range(TAPS):
                total = total + window[tap] * frames[s + tap]
            filtered.append(total.astype(jnp.bfloat16))
        filtered = jnp.stack(filtered)
        spectra.append(
            jnp.einsum(
                "srn,ndk->dsrk",
                filtered,
                jnp.asarray(table).reshape(NF, homes, per_dev),
                preferred_element_type=jnp.float32,
            ).astype(jnp.bfloat16)
        )
    outgoing = jnp.stack(spectra, axis=1)
    incoming = lax.all_to_all(outgoing, ("chan", "blk"), split_axis=0, concat_axis=0, tiled=True)
    station = incoming.reshape(homes * count, spectra_dev, rows, per_dev)
    place = (jnp.arange(homes, dtype=jnp.int32)[:, None] * count + rank).reshape(-1)
    pick = jnp.take(place, block_pairs)
    left = jnp.take(station, pick[:, 0], axis=0)
    right = jnp.take(station, pick[:, 1], axis=0)
    half = per_dev // 2
    turned = jnp.concatenate([-right[..., half:], right[..., :half]], axis=-1)
    partner = jnp.stack([right, turned], axis=0)
    return jnp.einsum("bsik,cbsjk->cbij", left, partner, preferred_element_type=jnp.float32)


def dense(voltages, history, block_pairs):
    antennas, feed_count, samples = voltages.shape
    spectra_dev = samples // NF
    frames = voltages.reshape(antennas, feed_count, spectra_dev, NF)
    tail_frames = frames[:, :, spectra_dev - (TAPS - 1) :, :]
    carried = from_behind(tail_frames, "pol", 1)
    stored = history.reshape(antennas, feed_count, TAPS - 1, NF)
    prior_frames = jnp.where(lax.axis_index("pol") == 0, stored, carried)
    signal = jnp.concatenate([prior_frames, frames], axis=2)
    window = prototype().reshape(TAPS, NF)
    filtered = jnp.zeros((antennas, feed_count, spectra_dev, NF), jnp.float32)
    for tap_index in range(TAPS):
        filtered = (
            filtered + window[tap_index] * signal[:, :, tap_index : tap_index + spectra_dev, :]
        )
    filtered = filtered.astype(jnp.bfloat16)
    n_chan = lax.axis_size("chan")
    n_blk = lax.axis_size("blk")
    turn_count = n_chan * n_blk
    dft_table = dft_rows()
    per_dev = dft_table.shape[2] // turn_count
    dft_table = dft_table.reshape(NF, 2, turn_count, per_dev)
    spectra = jnp.einsum(
        "afsn,nrdc->dafsrc", filtered, dft_table, preferred_element_type=jnp.float32
    ).astype(jnp.bfloat16)
    contract_len = spectra_dev * 2 * per_dev
    outgoing = spectra.reshape(turn_count, antennas, feed_count, contract_len)
    incoming = lax.all_to_all(outgoing, ("chan", "blk"), split_axis=0, concat_axis=0, tiled=True)
    block_rows = ABLK * feed_count
    block_count = block_pairs.shape[0]
    station = incoming.reshape(-1, block_rows, contract_len)
    left_rows = jnp.take(station, block_pairs[:, 0], axis=0)
    right_rows = jnp.take(station, block_pairs[:, 1], axis=0)
    right_split = right_rows.reshape(block_count, block_rows, spectra_dev, 2, per_dev)
    turned = jnp.stack([-right_split[:, :, :, 1, :], right_split[:, :, :, 0, :]], axis=3)
    turned = turned.reshape(block_count, block_rows, contract_len)
    partner = jnp.stack([right_rows, turned], axis=0)
    return jnp.einsum("bik,cbjk->cbij", left_rows, partner, preferred_element_type=jnp.float32)


def shards(voltages, history, block_pairs, owner_map, weights):
    antennas, feed_count, samples = voltages.shape
    spectra_dev = samples // NF
    n_chan = lax.axis_size("chan")
    n_blk = lax.axis_size("blk")
    n_pol = lax.axis_size("pol")
    per_dev = NF // 2 // (n_chan * n_blk)
    block_rows = ABLK * feed_count
    block_count = block_pairs.shape[0]
    if antennas % ABLK == 0:
        _, _, most = listed_blocks(block_pairs, n_chan * n_blk, antennas // ABLK)
        counts = [c for c in (1, 2, antennas // ABLK) if c <= antennas // ABLK]
        choice = sum((most > c).astype(jnp.int32) for c in counts[:-1])
        products = lax.switch(
            choice,
            [partial(compact, c) for c in counts],
            voltages,
            history,
            block_pairs,
            owner_map,
            weights,
        )
    else:
        products = dense(voltages, history, block_pairs)
    count_terms = per_dev * n_blk * spectra_dev * n_pol
    factor = weights.astype(jnp.float32) / math.sqrt(count_terms)
    capacity = min(CAP, block_count - 1)
    parts_each = 2 // n_pol
    my_owner = jnp.reshape(lax.axis_index("blk"), (1,))
    mine_matched, mine_source, mine_filled = slot_sources(owner_map, my_owner, capacity)
    part_steps = jnp.arange(parts_each, dtype=jnp.int32)
    all_owners = jnp.arange(n_blk, dtype=jnp.int32)
    matched, source, filled = slot_sources(owner_map, all_owners, capacity)
    component = jnp.arange(n_pol, dtype=jnp.int32)[:, None] * parts_each + part_steps[None, :]
    take_index = component[None, :, None, :] * block_count + source[:, None, :, None]
    keep = jnp.broadcast_to(filled[:, None, :, None], take_index.shape).reshape(-1)
    flat_terms = products.reshape(2 * block_count, block_rows, block_rows)
    gathered = jnp.take(flat_terms, take_index.reshape(-1), axis=0)
    send_buffer = jnp.where(keep[:, None, None], gathered, 0.0)
    send_buffer = send_buffer.reshape(n_blk * n_pol, capacity * parts_each, block_rows, block_rows)
    received = lax.all_to_all(send_buffer, ("blk", "pol"), split_axis=0, concat_axis=0, tiled=True)
    summed = jnp.sum(received, axis=0)
    slot_scale = jnp.sum(jnp.where(mine_matched[0], factor[None, :], 0.0), axis=1)
    result = (
        summed.reshape(capacity, parts_each, block_rows, block_rows)
        * slot_scale[:, None, None, None]
    )
    return result.reshape(1, capacity, parts_each, block_rows, block_rows)


def solution(mesh):
    in_specs = (
        P(("group", "chan", "blk"), None, "pol"),
        P(("group", "chan", "blk"), None, None),
        P(),
        P(),
        P(),
    )
    out_specs = P(("group", "chan"), "blk", "pol", None, None)
    return jax.shard_map(shards, mesh=mesh, in_specs=in_specs, out_specs=out_specs, check_vma=False)
```

```python
import math
from functools import partial

import jax
import jax.numpy as jnp
import numpy as np
from jax import lax
from jax.experimental import pallas as pl
from jax.experimental.pallas import tpu as pltpu
from jax.sharding import PartitionSpec as P

ABLK = 64
NF = 2048
TAPS = 8
CAP = 4


def from_behind(block, axis, distance):
    devices = range(lax.axis_size(axis))
    route = [(i - distance, i) for i in devices if i - distance in devices]
    return lax.ppermute(block, axis, route)


def prototype():
    length = TAPS * NF
    position = jnp.arange(length, dtype=jnp.float32)
    taper_win = 0.54 - 0.46 * jnp.cos(2.0 * math.pi / (length - 1) * position)
    raw_taps = jnp.sinc((position - length / 2) / NF) * taper_win
    return raw_taps / jnp.sqrt(jnp.sum(raw_taps * raw_taps) / NF)


def dft_rows():
    sample = jnp.arange(NF, dtype=jnp.int32)[:, None]
    channel = jnp.arange(NF // 2, dtype=jnp.int32)[None, :]
    phases = (sample * channel % NF).astype(jnp.float32) * (2.0 * math.pi / NF)
    normalize = 1.0 / math.sqrt(NF)
    cosine = (jnp.cos(phases) * normalize).astype(jnp.bfloat16)
    sine_part = (jnp.sin(phases) * -normalize).astype(jnp.bfloat16)
    return jnp.stack([cosine, sine_part], axis=1)


def slot_sources(owner_map, owners, capacity):
    blocks = owner_map.shape[0]
    ordinal = jnp.arange(blocks, dtype=jnp.int32)
    same_owner = owner_map[None, :] == owner_map[:, None]
    earlier = ordinal[None, :] < ordinal[:, None]
    ranking = jnp.sum(jnp.logical_and(same_owner, earlier), axis=1)
    position = jnp.arange(capacity, dtype=jnp.int32)
    matched = jnp.logical_and(
        owner_map[None, None, :] == owners[:, None, None],
        ranking[None, None, :] == position[None, :, None],
    )
    source = jnp.sum(jnp.where(matched, ordinal[None, None, :], 0), axis=2)
    filled = jnp.any(matched, axis=2)
    return (matched, source, filled)


def constants(pieces):
    length = TAPS * NF
    position = np.arange(length, dtype=np.float64)
    taper_win = 0.54 - 0.46 * np.cos(2.0 * math.pi / (length - 1) * position)
    raw_taps = np.sinc((position - length / 2) / NF) * taper_win
    window = raw_taps / np.sqrt(np.sum(raw_taps * raw_taps) / NF)
    sample = np.arange(NF, dtype=np.int64)[:, None]
    channel = np.arange(NF // 2, dtype=np.int64)[None, :]
    phases = (sample * channel % NF).astype(np.float32) * np.float32(2.0 * math.pi / NF)
    phases = phases.astype(np.float64)
    normalize = np.float32(1.0 / math.sqrt(NF))
    cosine = np.cos(phases).astype(np.float32) * normalize
    sine = np.sin(phases).astype(np.float32) * -normalize
    table = np.stack([cosine, sine], axis=1).reshape(NF, 2, pieces, -1)
    table = table.transpose(0, 2, 1, 3).reshape(NF, -1)
    return window.astype(np.float32).reshape(TAPS, NF), table.astype(jnp.bfloat16)


def listed_blocks(block_pairs, homes, held):
    listed = jnp.any(
        block_pairs.reshape(-1)[:, None] == jnp.arange(homes * held, dtype=jnp.int32)[None, :],
        axis=0,
    ).reshape(homes, held)
    rank = jnp.cumsum(listed.astype(jnp.int32), axis=1) - 1
    most = jnp.max(rank[:, -1]) + 1
    return listed, rank, most


def select_kernel(local, source, target):
    target[...] = source[...].reshape(target.shape)


def select(source, local):
    _, feeds, samples = source.shape
    count = local.shape[0]
    step = 16
    chunks = ABLK // step
    return pl.pallas_call(
        select_kernel,
        grid_spec=pltpu.PrefetchScalarGridSpec(
            num_scalar_prefetch=1,
            grid=(count, chunks),
            in_specs=[
                pl.BlockSpec((step, feeds, samples), lambda k, c, local: (local[k] * chunks + c, 0, 0))
            ],
            out_specs=pl.BlockSpec((step * feeds, samples), lambda k, c, local: (k * chunks + c, 0)),
        ),
        out_shape=jax.ShapeDtypeStruct((count * ABLK * feeds, samples), source.dtype),
        compiler_params=pltpu.CompilerParams(vmem_limit_bytes=48 * 2**20),
        cost_estimate=pl.CostEstimate(
            flops=0, bytes_accessed=4 * count * ABLK * feeds * samples, transcendentals=0
        ),
    )(local, source)


def channelize_kernel(half, fresh, older, carried, window, table, spectra, filtered):
    rows, samples = fresh.shape
    count = samples // NF
    row_step, step = 16, 256

    @pl.when(pl.program_id(1) == 0)
    def _():
        first = half[0] == 0

        @pl.loop(0, rows // row_step)
        def _(r):
            at_rows = pl.ds(pl.multiple_of(r * row_step, row_step), row_step)

            @pl.loop(0, NF // step)
            def _(c):
                col = pl.multiple_of(c * step, step)
                taps = [window[pl.ds(t, 1), pl.ds(col, step)] for t in range(TAPS)]
                frames = []
                for i in range(TAPS - 1):
                    cols = pl.ds(col + i * NF, step)
                    was = older[at_rows, cols].astype(jnp.float32)
                    got = carried[at_rows, cols].astype(jnp.float32)
                    frames.append(jnp.where(first, was, got))
                for i in range(count):
                    cols = pl.ds(col + i * NF, step)
                    frames.append(fresh[at_rows, cols].astype(jnp.float32))
                for s in range(count):
                    total = taps[0] * frames[s]
                    for t in range(1, TAPS):
                        total = total + taps[t] * frames[s + t]
                    spot = pl.ds(pl.multiple_of(s * rows + r * row_step, row_step), row_step)
                    filtered[spot, pl.ds(col, step)] = total.astype(jnp.bfloat16)

    spectra[0, 0] = jnp.dot(
        filtered[...], table[...], preferred_element_type=jnp.float32
    ).astype(jnp.bfloat16)


def channelize(half, fresh, older, carried, window, table, count, homes):
    rows = fresh.shape[0] // count
    samples = fresh.shape[1]
    tall = rows * (samples // NF)
    per_dev = NF // homes
    past = older.shape[1]
    return pl.pallas_call(
        channelize_kernel,
        grid_spec=pltpu.PrefetchScalarGridSpec(
            num_scalar_prefetch=1,
            grid=(count, homes),
            in_specs=[
                pl.BlockSpec((rows, samples), lambda k, d, half: (k, 0)),
                pl.BlockSpec((rows, past), lambda k, d, half: (k, 0)),
                pl.BlockSpec((rows, past), lambda k, d, half: (k, 0)),
                pl.BlockSpec((TAPS, NF), lambda k, d, half: (0, 0)),
                pl.BlockSpec((NF, per_dev), lambda k, d, half: (0, d)),
            ],
            out_specs=pl.BlockSpec((1, 1, tall, per_dev), lambda k, d, half: (d, k, 0, 0)),
            scratch_shapes=[pltpu.VMEM((tall, NF), jnp.bfloat16)],
        ),
        out_shape=jax.ShapeDtypeStruct((homes, count, tall, per_dev), jnp.bfloat16),
        compiler_params=pltpu.CompilerParams(vmem_limit_bytes=56 * 2**20),
        cost_estimate=pl.CostEstimate(
            flops=2 * count * tall * NF * NF,
            bytes_accessed=16 * 2**20 * count,
            transcendentals=0,
        ),
    )(half, fresh, older, carried, window, table)


def correlate_kernel(
    homes, n_blk, count, blocks, capacity,
    places, factors, outgoing, result,
    station, products, summed, from_pol, to_blk, from_blk, send, receive, own,
):
    chan, blk, pol = (lax.axis_index(a) for a in ("chan", "blk", "pol"))
    me = chan * n_blk + blk
    rows = products.shape[-1]
    frames = outgoing.shape[2] // rows

    def member(other):
        return {"chan": other // n_blk, "blk": lax.rem(other, n_blk)}

    barrier = pltpu.get_barrier_semaphore()
    for step in range(1, homes):
        pl.semaphore_signal(
            barrier, inc=1, device_id=member(lax.rem(me + step, homes)),
            device_id_type=pl.DeviceIdType.MESH,
        )
    pl.semaphore_signal(
        barrier, inc=1, device_id={"pol": 1 - pol}, device_id_type=pl.DeviceIdType.MESH
    )
    pl.semaphore_wait(barrier, homes)

    copies = []
    for index, step in enumerate((4, 3, 5, 2, 6, 1, 7) if homes == 8 else range(1, homes)):
        other = lax.rem(me + step, homes)
        copy = pltpu.make_async_remote_copy(
            src_ref=outgoing.at[other],
            dst_ref=station.at[me],
            send_sem=send.at[index],
            recv_sem=receive.at[index],
            device_id=member(other),
            device_id_type=pl.DeviceIdType.MESH,
        )
        copy.start()
        copies.append(copy)
    mine = pltpu.make_async_copy(outgoing.at[me], station.at[me], own)
    mine.start()
    mine.wait()
    for copy in copies:
        copy.wait()

    half = station.shape[-1] // 2
    over = (((1,), (1,)), ((), ()))
    for b in range(blocks):
        left_home, left_at = places[b], places[blocks + b]
        right_home, right_at = places[2 * blocks + b], places[3 * blocks + b]
        real = jnp.zeros((rows, rows), jnp.float32)
        imag = jnp.zeros((rows, rows), jnp.float32)
        for s in range(frames):
            span = pl.ds(s * rows, rows)
            left = station[left_home, left_at, span, :]
            right = station[right_home, right_at, span, :]
            turned = jnp.concatenate([-right[:, half:], right[:, :half]], axis=1)
            real += lax.dot_general(left, right, over, preferred_element_type=jnp.float32)
            imag += lax.dot_general(left, turned, over, preferred_element_type=jnp.float32)
        products[0, b] = real
        products[1, b] = imag

    last = homes - 1
    swap = pltpu.make_async_remote_copy(
        src_ref=products.at[1 - pol],
        dst_ref=from_pol,
        send_sem=send.at[last],
        recv_sem=receive.at[last],
        device_id={"pol": 1 - pol},
        device_id_type=pl.DeviceIdType.MESH,
    )
    swap.start()
    swap.wait()
    summed[...] = products[pol] + from_pol[...]
    for c in range(capacity):
        to_blk[c] = summed[places[4 * blocks + capacity + c]]
    swap = pltpu.make_async_remote_copy(
        src_ref=to_blk,
        dst_ref=from_blk,
        send_sem=send.at[last + 1],
        recv_sem=receive.at[last + 1],
        device_id={"blk": 1 - blk},
        device_id_type=pl.DeviceIdType.MESH,
    )
    swap.start()
    swap.wait()
    for c in range(capacity):
        result[c] = (summed[places[4 * blocks + c]] + from_blk[c]) * factors[c]


def correlate(places, factors, outgoing, blocks, n_blk):
    homes, count, tall, per_dev = outgoing.shape
    capacity = factors.shape[0]
    rows = 2 * ABLK
    square = lambda *lead: pltpu.VMEM((*lead, rows, rows), jnp.float32)
    return pl.pallas_call(
        partial(correlate_kernel, homes, n_blk, count, blocks, capacity),
        out_shape=jax.ShapeDtypeStruct((capacity, rows, rows), jnp.float32),
        in_specs=[
            pl.BlockSpec(memory_space=pltpu.SMEM),
            pl.BlockSpec(memory_space=pltpu.SMEM),
            pl.BlockSpec(memory_space=pl.ANY),
        ],
        out_specs=pl.BlockSpec(memory_space=pltpu.VMEM),
        scratch_shapes=[
            pltpu.VMEM(outgoing.shape, jnp.bfloat16),
            square(2, blocks),
            square(blocks),
            square(blocks),
            square(capacity),
            square(capacity),
            pltpu.SemaphoreType.DMA((homes + 1,)),
            pltpu.SemaphoreType.DMA((homes + 1,)),
            pltpu.SemaphoreType.DMA,
        ],
        compiler_params=pltpu.CompilerParams(
            collective_id=count, has_side_effects=True, vmem_limit_bytes=48 * 2**20
        ),
    )(places, factors, outgoing)


def listed_branch(count, table, voltages, history, block_pairs, mine, rank, sources, factors):
    homes = lax.axis_size("chan") * lax.axis_size("blk")
    held = voltages.shape[0] // ABLK
    window, _ = constants(homes)
    order = jnp.arange(count, dtype=jnp.int32)
    local = jnp.sum(
        jnp.where(mine[None, :] == order[:, None], jnp.arange(held, dtype=jnp.int32)[None, :], 0),
        axis=1,
    ).astype(jnp.int32)
    fresh = select(voltages, local)
    carried = from_behind(fresh[:, fresh.shape[1] - (TAPS - 1) * NF :], "pol", 1)
    older = select(history, local)
    half = lax.axis_index("pol").astype(jnp.int32).reshape(1)
    outgoing = channelize(half, fresh, older, carried, jnp.asarray(window), table, count, homes)
    pairs = block_pairs.T.astype(jnp.int32)
    home = pairs // held
    at = jnp.take(rank.reshape(-1), pairs)
    places = jnp.concatenate([home[0], at[0], home[1], at[1], sources]).astype(jnp.int32)
    return correlate(places, factors, outgoing, block_pairs.shape[0], lax.axis_size("blk"))


def listed_only(voltages, history, block_pairs, owner_map, weights):
    antennas, feed_count, samples = voltages.shape
    n_chan, n_blk, n_pol = (lax.axis_size(a) for a in ("chan", "blk", "pol"))
    homes = n_chan * n_blk
    held = antennas // ABLK
    blocks = block_pairs.shape[0]
    blk = lax.axis_index("blk")
    listed, rank, most = listed_blocks(block_pairs, homes, held)
    me = lax.axis_index("chan") * n_blk + blk
    mine = lax.dynamic_index_in_dim(jnp.where(listed, rank, -1), me, 0, keepdims=False)
    capacity = min(CAP, blocks - 1)
    owners = jnp.stack([blk, 1 - blk]).astype(jnp.int32)
    matched, source, filled = slot_sources(owner_map, owners, capacity)
    count_terms = NF // 2 // n_chan * (samples // NF) * n_pol
    factor = weights.astype(jnp.float32) / math.sqrt(count_terms)
    factors = jnp.sum(jnp.where(matched[0], factor[None, :], 0.0), axis=1)
    counts = [c for c in (1, 2, held) if c <= held]
    choice = sum((most > c).astype(jnp.int32) for c in counts[:-1])
    _, table = constants(homes)
    result = lax.switch(
        choice,
        [partial(listed_branch, c) for c in counts],
        jnp.asarray(table),
        voltages,
        history,
        block_pairs,
        mine,
        rank,
        source.reshape(-1).astype(jnp.int32),
        factors,
    )
    rows = ABLK * feed_count
    return result.reshape(1, capacity, 1, rows, rows)


def dense(voltages, history, block_pairs):
    antennas, feed_count, samples = voltages.shape
    spectra_dev = samples // NF
    frames = voltages.reshape(antennas, feed_count, spectra_dev, NF)
    tail_frames = frames[:, :, spectra_dev - (TAPS - 1) :, :]
    carried = from_behind(tail_frames, "pol", 1)
    stored = history.reshape(antennas, feed_count, TAPS - 1, NF)
    prior_frames = jnp.where(lax.axis_index("pol") == 0, stored, carried)
    signal = jnp.concatenate([prior_frames, frames], axis=2)
    window = prototype().reshape(TAPS, NF)
    filtered = jnp.zeros((antennas, feed_count, spectra_dev, NF), jnp.float32)
    for tap_index in range(TAPS):
        filtered = (
            filtered + window[tap_index] * signal[:, :, tap_index : tap_index + spectra_dev, :]
        )
    filtered = filtered.astype(jnp.bfloat16)
    n_chan = lax.axis_size("chan")
    n_blk = lax.axis_size("blk")
    turn_count = n_chan * n_blk
    dft_table = dft_rows()
    per_dev = dft_table.shape[2] // turn_count
    dft_table = dft_table.reshape(NF, 2, turn_count, per_dev)
    spectra = jnp.einsum(
        "afsn,nrdc->dafsrc", filtered, dft_table, preferred_element_type=jnp.float32
    ).astype(jnp.bfloat16)
    contract_len = spectra_dev * 2 * per_dev
    outgoing = spectra.reshape(turn_count, antennas, feed_count, contract_len)
    incoming = lax.all_to_all(outgoing, ("chan", "blk"), split_axis=0, concat_axis=0, tiled=True)
    block_rows = ABLK * feed_count
    block_count = block_pairs.shape[0]
    station = incoming.reshape(-1, block_rows, contract_len)
    left_rows = jnp.take(station, block_pairs[:, 0], axis=0)
    right_rows = jnp.take(station, block_pairs[:, 1], axis=0)
    right_split = right_rows.reshape(block_count, block_rows, spectra_dev, 2, per_dev)
    turned = jnp.stack([-right_split[:, :, :, 1, :], right_split[:, :, :, 0, :]], axis=3)
    turned = turned.reshape(block_count, block_rows, contract_len)
    partner = jnp.stack([right_rows, turned], axis=0)
    return jnp.einsum("bik,cbjk->cbij", left_rows, partner, preferred_element_type=jnp.float32)


def shards(voltages, history, block_pairs, owner_map, weights):
    antennas, feed_count, samples = voltages.shape
    spectra_dev = samples // NF
    if antennas % ABLK == 0 and lax.axis_size("blk") == 2 and lax.axis_size("pol") == 2:
        return listed_only(voltages, history, block_pairs, owner_map, weights)
    n_chan = lax.axis_size("chan")
    n_blk = lax.axis_size("blk")
    n_pol = lax.axis_size("pol")
    per_dev = NF // 2 // (n_chan * n_blk)
    block_rows = ABLK * feed_count
    block_count = block_pairs.shape[0]
    products = dense(voltages, history, block_pairs)
    count_terms = per_dev * n_blk * spectra_dev * n_pol
    factor = weights.astype(jnp.float32) / math.sqrt(count_terms)
    capacity = min(CAP, block_count - 1)
    parts_each = 2 // n_pol
    my_owner = jnp.reshape(lax.axis_index("blk"), (1,))
    mine_matched, mine_source, mine_filled = slot_sources(owner_map, my_owner, capacity)
    part_steps = jnp.arange(parts_each, dtype=jnp.int32)
    all_owners = jnp.arange(n_blk, dtype=jnp.int32)
    matched, source, filled = slot_sources(owner_map, all_owners, capacity)
    component = jnp.arange(n_pol, dtype=jnp.int32)[:, None] * parts_each + part_steps[None, :]
    take_index = component[None, :, None, :] * block_count + source[:, None, :, None]
    keep = jnp.broadcast_to(filled[:, None, :, None], take_index.shape).reshape(-1)
    flat_terms = products.reshape(2 * block_count, block_rows, block_rows)
    gathered = jnp.take(flat_terms, take_index.reshape(-1), axis=0)
    send_buffer = jnp.where(keep[:, None, None], gathered, 0.0)
    send_buffer = send_buffer.reshape(n_blk * n_pol, capacity * parts_each, block_rows, block_rows)
    received = lax.all_to_all(send_buffer, ("blk", "pol"), split_axis=0, concat_axis=0, tiled=True)
    summed = jnp.sum(received, axis=0)
    slot_scale = jnp.sum(jnp.where(mine_matched[0], factor[None, :], 0.0), axis=1)
    result = (
        summed.reshape(capacity, parts_each, block_rows, block_rows)
        * slot_scale[:, None, None, None]
    )
    return result.reshape(1, capacity, parts_each, block_rows, block_rows)


def solution(mesh):
    in_specs = (
        P(("group", "chan", "blk"), None, "pol"),
        P(("group", "chan", "blk"), None, None),
        P(),
        P(),
        P(),
    )
    out_specs = P(("group", "chan"), "blk", "pol", None, None)
    return jax.shard_map(shards, mesh=mesh, in_specs=in_specs, out_specs=out_specs, check_vma=False)
```

```python
import math
from functools import partial

import jax
import jax.numpy as jnp
import numpy as np
from jax import lax
from jax.experimental import pallas as pl
from jax.experimental.pallas import tpu as pltpu
from jax.sharding import PartitionSpec as P

ABLK = 64
NF = 2048
TAPS = 8
CAP = 4


def from_behind(block, axis, distance):
    devices = range(lax.axis_size(axis))
    route = [(i - distance, i) for i in devices if i - distance in devices]
    return lax.ppermute(block, axis, route)


def prototype():
    length = TAPS * NF
    position = jnp.arange(length, dtype=jnp.float32)
    taper_win = 0.54 - 0.46 * jnp.cos(2.0 * math.pi / (length - 1) * position)
    raw_taps = jnp.sinc((position - length / 2) / NF) * taper_win
    return raw_taps / jnp.sqrt(jnp.sum(raw_taps * raw_taps) / NF)


def dft_rows():
    sample = jnp.arange(NF, dtype=jnp.int32)[:, None]
    channel = jnp.arange(NF // 2, dtype=jnp.int32)[None, :]
    phases = (sample * channel % NF).astype(jnp.float32) * (2.0 * math.pi / NF)
    normalize = 1.0 / math.sqrt(NF)
    cosine = (jnp.cos(phases) * normalize).astype(jnp.bfloat16)
    sine_part = (jnp.sin(phases) * -normalize).astype(jnp.bfloat16)
    return jnp.stack([cosine, sine_part], axis=1)


def slot_sources(owner_map, owners, capacity):
    blocks = owner_map.shape[0]
    ordinal = jnp.arange(blocks, dtype=jnp.int32)
    same_owner = owner_map[None, :] == owner_map[:, None]
    earlier = ordinal[None, :] < ordinal[:, None]
    ranking = jnp.sum(jnp.logical_and(same_owner, earlier), axis=1)
    position = jnp.arange(capacity, dtype=jnp.int32)
    matched = jnp.logical_and(
        owner_map[None, None, :] == owners[:, None, None],
        ranking[None, None, :] == position[None, :, None],
    )
    source = jnp.sum(jnp.where(matched, ordinal[None, None, :], 0), axis=2)
    filled = jnp.any(matched, axis=2)
    return (matched, source, filled)


def constants(pieces):
    length = TAPS * NF
    position = np.arange(length, dtype=np.float64)
    taper_win = 0.54 - 0.46 * np.cos(2.0 * math.pi / (length - 1) * position)
    raw_taps = np.sinc((position - length / 2) / NF) * taper_win
    window = raw_taps / np.sqrt(np.sum(raw_taps * raw_taps) / NF)
    sample = np.arange(NF, dtype=np.int64)[:, None]
    channel = np.arange(NF // 2, dtype=np.int64)[None, :]
    phases = (sample * channel % NF).astype(np.float32) * np.float32(2.0 * math.pi / NF)
    phases = phases.astype(np.float64)
    normalize = np.float32(1.0 / math.sqrt(NF))
    cosine = np.cos(phases).astype(np.float32) * normalize
    sine = np.sin(phases).astype(np.float32) * -normalize
    table = np.stack([cosine, sine], axis=1).reshape(NF, 2, pieces, -1)
    table = table.transpose(0, 2, 1, 3).reshape(NF, -1)
    return window.astype(np.float32).reshape(TAPS, NF), table.astype(jnp.bfloat16)


def listed_blocks(block_pairs, homes, held):
    listed = jnp.any(
        block_pairs.reshape(-1)[:, None] == jnp.arange(homes * held, dtype=jnp.int32)[None, :],
        axis=0,
    ).reshape(homes, held)
    rank = jnp.cumsum(listed.astype(jnp.int32), axis=1) - 1
    most = jnp.max(rank[:, -1]) + 1
    return listed, rank, most


def select_kernel(local, source, target):
    target[...] = source[...].reshape(target.shape)


def select(source, local):
    _, feeds, samples = source.shape
    count = local.shape[0]
    step = 16
    chunks = ABLK // step
    return pl.pallas_call(
        select_kernel,
        grid_spec=pltpu.PrefetchScalarGridSpec(
            num_scalar_prefetch=1,
            grid=(count, chunks),
            in_specs=[
                pl.BlockSpec((step, feeds, samples), lambda k, c, local: (local[k] * chunks + c, 0, 0))
            ],
            out_specs=pl.BlockSpec((step * feeds, samples), lambda k, c, local: (k * chunks + c, 0)),
        ),
        out_shape=jax.ShapeDtypeStruct((count * ABLK * feeds, samples), source.dtype),
        compiler_params=pltpu.CompilerParams(vmem_limit_bytes=48 * 2**20),
        cost_estimate=pl.CostEstimate(
            flops=0, bytes_accessed=4 * count * ABLK * feeds * samples, transcendentals=0
        ),
    )(local, source)


def channelize_kernel(half, fresh, older, carried, window, table, spectra, filtered):
    rows, samples = fresh.shape
    count = samples // NF
    row_step, step = 16, 256

    @pl.when(pl.program_id(1) == 0)
    def _():
        first = half[0] == 0

        @pl.loop(0, rows // row_step)
        def _(r):
            at_rows = pl.ds(pl.multiple_of(r * row_step, row_step), row_step)

            @pl.loop(0, NF // step)
            def _(c):
                col = pl.multiple_of(c * step, step)
                taps = [window[pl.ds(t, 1), pl.ds(col, step)] for t in range(TAPS)]
                frames = []
                for i in range(TAPS - 1):
                    cols = pl.ds(col + i * NF, step)
                    was = older[at_rows, cols].astype(jnp.float32)
                    got = carried[at_rows, cols].astype(jnp.float32)
                    frames.append(jnp.where(first, was, got))
                for i in range(count):
                    cols = pl.ds(col + i * NF, step)
                    frames.append(fresh[at_rows, cols].astype(jnp.float32))
                for s in range(count):
                    total = taps[0] * frames[s]
                    for t in range(1, TAPS):
                        total = total + taps[t] * frames[s + t]
                    spot = pl.ds(pl.multiple_of(s * rows + r * row_step, row_step), row_step)
                    filtered[spot, pl.ds(col, step)] = total.astype(jnp.bfloat16)

    spectra[0, 0] = jnp.dot(
        filtered[...], table[...], preferred_element_type=jnp.float32
    ).astype(jnp.bfloat16)


def channelize(half, fresh, older, carried, window, table, count, homes):
    rows = fresh.shape[0] // count
    samples = fresh.shape[1]
    tall = rows * (samples // NF)
    per_dev = NF // homes
    past = older.shape[1]
    return pl.pallas_call(
        channelize_kernel,
        grid_spec=pltpu.PrefetchScalarGridSpec(
            num_scalar_prefetch=1,
            grid=(count, homes),
            in_specs=[
                pl.BlockSpec((rows, samples), lambda k, d, half: (k, 0)),
                pl.BlockSpec((rows, past), lambda k, d, half: (k, 0)),
                pl.BlockSpec((rows, past), lambda k, d, half: (k, 0)),
                pl.BlockSpec((TAPS, NF), lambda k, d, half: (0, 0)),
                pl.BlockSpec((NF, per_dev), lambda k, d, half: (0, d)),
            ],
            out_specs=pl.BlockSpec((1, 1, tall, per_dev), lambda k, d, half: (d, k, 0, 0)),
            scratch_shapes=[pltpu.VMEM((tall, NF), jnp.bfloat16)],
        ),
        out_shape=jax.ShapeDtypeStruct((homes, count, tall, per_dev), jnp.bfloat16),
        compiler_params=pltpu.CompilerParams(vmem_limit_bytes=56 * 2**20),
        cost_estimate=pl.CostEstimate(
            flops=2 * count * tall * NF * NF,
            bytes_accessed=16 * 2**20 * count,
            transcendentals=0,
        ),
    )(half, fresh, older, carried, window, table)


def correlate_kernel(
    homes, n_blk, loads, blocks, capacity,
    places, factors, outgoing, result,
    station, products, summed, from_pol, to_blk, from_blk, send, receive, own,
):
    chan, blk, pol = (lax.axis_index(a) for a in ("chan", "blk", "pol"))
    me = chan * n_blk + blk
    rows = products.shape[-1]
    frames = outgoing.shape[2] // rows

    def member(other):
        return {"chan": other // n_blk, "blk": lax.rem(other, n_blk)}

    barrier = pltpu.get_barrier_semaphore()
    for step in range(1, homes):
        pl.semaphore_signal(
            barrier, inc=1, device_id=member(lax.rem(me + step, homes)),
            device_id_type=pl.DeviceIdType.MESH,
        )
    pl.semaphore_signal(
        barrier, inc=1, device_id={"pol": 1 - pol}, device_id_type=pl.DeviceIdType.MESH
    )
    pl.semaphore_wait(barrier, homes)

    def loaded(device, slot):
        full = [d for d in range(homes) if loads[d] > slot]
        if len(full) == homes:
            return None
        yes = device == full[0]
        for d in full[1:]:
            yes = jnp.logical_or(yes, device == d)
        return yes

    def when(yes, action):
        if yes is None:
            action()
        else:
            pl.when(yes)(action)

    copies = []
    count = max(loads)
    steps = (4, 3, 5, 2, 6, 1, 7) if homes == 8 else tuple(range(1, homes))
    for slot in range(count):
        sending = loaded(me, slot)
        for index, step in enumerate(steps):
            other = lax.rem(me + step, homes)
            copy = pltpu.make_async_remote_copy(
                src_ref=outgoing.at[other, slot],
                dst_ref=station.at[me, slot],
                send_sem=send.at[slot * homes + index],
                recv_sem=receive.at[slot * homes + index],
                device_id=member(other),
                device_id_type=pl.DeviceIdType.MESH,
            )
            when(sending, copy.start)
            coming = loaded(lax.rem(me - step + homes, homes), slot)
            copies.append((copy, sending, coming))
    mine = pltpu.make_async_copy(outgoing.at[me], station.at[me], own)
    mine.start()
    mine.wait()
    for copy, sending, coming in copies:
        when(sending, copy.wait_send)
        when(coming, copy.wait_recv)

    half = station.shape[-1] // 2
    over = (((1,), (1,)), ((), ()))
    for b in range(blocks):
        left_home, left_at = places[b], places[blocks + b]
        right_home, right_at = places[2 * blocks + b], places[3 * blocks + b]
        real = jnp.zeros((rows, rows), jnp.float32)
        imag = jnp.zeros((rows, rows), jnp.float32)
        for s in range(frames):
            span = pl.ds(s * rows, rows)
            left = station[left_home, left_at, span, :]
            right = station[right_home, right_at, span, :]
            turned = jnp.concatenate([-right[:, half:], right[:, :half]], axis=1)
            real += lax.dot_general(left, right, over, preferred_element_type=jnp.float32)
            imag += lax.dot_general(left, turned, over, preferred_element_type=jnp.float32)
        products[0, b] = real
        products[1, b] = imag

    last = count * homes
    swap = pltpu.make_async_remote_copy(
        src_ref=products.at[1 - pol],
        dst_ref=from_pol,
        send_sem=send.at[last],
        recv_sem=receive.at[last],
        device_id={"pol": 1 - pol},
        device_id_type=pl.DeviceIdType.MESH,
    )
    swap.start()
    swap.wait()
    summed[...] = products[pol] + from_pol[...]
    for c in range(capacity):
        to_blk[c] = summed[places[4 * blocks + capacity + c]]
    swap = pltpu.make_async_remote_copy(
        src_ref=to_blk,
        dst_ref=from_blk,
        send_sem=send.at[last + 1],
        recv_sem=receive.at[last + 1],
        device_id={"blk": 1 - blk},
        device_id_type=pl.DeviceIdType.MESH,
    )
    swap.start()
    swap.wait()
    for c in range(capacity):
        result[c] = (summed[places[4 * blocks + c]] + from_blk[c]) * factors[c]


def correlate(loads, serial, blocks, n_blk, places, factors, outgoing):
    homes, count, tall, per_dev = outgoing.shape
    capacity = factors.shape[0]
    rows = 2 * ABLK
    square = lambda *lead: pltpu.VMEM((*lead, rows, rows), jnp.float32)
    return pl.pallas_call(
        partial(correlate_kernel, homes, n_blk, loads, blocks, capacity),
        out_shape=jax.ShapeDtypeStruct((capacity, rows, rows), jnp.float32),
        in_specs=[
            pl.BlockSpec(memory_space=pltpu.SMEM),
            pl.BlockSpec(memory_space=pltpu.SMEM),
            pl.BlockSpec(memory_space=pl.ANY),
        ],
        out_specs=pl.BlockSpec(memory_space=pltpu.VMEM),
        scratch_shapes=[
            pltpu.VMEM(outgoing.shape, jnp.bfloat16),
            square(2, blocks),
            square(blocks),
            square(blocks),
            square(capacity),
            square(capacity),
            pltpu.SemaphoreType.DMA((count * homes + 2,)),
            pltpu.SemaphoreType.DMA((count * homes + 2,)),
            pltpu.SemaphoreType.DMA,
        ],
        compiler_params=pltpu.CompilerParams(
            collective_id=serial, has_side_effects=True, vmem_limit_bytes=48 * 2**20
        ),
    )(places, factors, outgoing)


def load_choices(homes, count):
    lighter = []
    if count == 2:
        lighter = [tuple(2 if d == e else 1 for d in range(homes)) for e in range(homes)]
    return lighter + [(count,) * homes]


def listed_branch(count, serial, table, voltages, history, block_pairs, listed, rank, sources, factors):
    homes = lax.axis_size("chan") * lax.axis_size("blk")
    held = voltages.shape[0] // ABLK
    window, _ = constants(homes)
    me = lax.axis_index("chan") * lax.axis_size("blk") + lax.axis_index("blk")
    mine = lax.dynamic_index_in_dim(jnp.where(listed, rank, -1), me, 0, keepdims=False)
    order = jnp.arange(count, dtype=jnp.int32)
    local = jnp.sum(
        jnp.where(mine[None, :] == order[:, None], jnp.arange(held, dtype=jnp.int32)[None, :], 0),
        axis=1,
    ).astype(jnp.int32)
    fresh = select(voltages, local)
    carried = from_behind(fresh[:, fresh.shape[1] - (TAPS - 1) * NF :], "pol", 1)
    older = select(history, local)
    half = lax.axis_index("pol").astype(jnp.int32).reshape(1)
    outgoing = channelize(half, fresh, older, carried, jnp.asarray(window), table, count, homes)
    pairs = block_pairs.T.astype(jnp.int32)
    home = pairs // held
    at = jnp.take(rank.reshape(-1), pairs)
    places = jnp.concatenate([home[0], at[0], home[1], at[1], sources]).astype(jnp.int32)
    choices = load_choices(homes, count)
    has = rank[:, -1] + 1
    fits = jnp.stack([jnp.all(has <= jnp.array(c, jnp.int32)) for c in choices])
    return lax.switch(
        jnp.argmax(fits).astype(jnp.int32),
        [
            partial(correlate, c, serial + i, block_pairs.shape[0], lax.axis_size("blk"))
            for i, c in enumerate(choices)
        ],
        places,
        factors,
        outgoing,
    )


def listed_only(voltages, history, block_pairs, owner_map, weights):
    antennas, feed_count, samples = voltages.shape
    n_chan, n_blk, n_pol = (lax.axis_size(a) for a in ("chan", "blk", "pol"))
    homes = n_chan * n_blk
    held = antennas // ABLK
    blocks = block_pairs.shape[0]
    blk = lax.axis_index("blk")
    listed, rank, most = listed_blocks(block_pairs, homes, held)
    capacity = min(CAP, blocks - 1)
    owners = jnp.stack([blk, 1 - blk]).astype(jnp.int32)
    matched, source, filled = slot_sources(owner_map, owners, capacity)
    count_terms = NF // 2 // n_chan * (samples // NF) * n_pol
    factor = weights.astype(jnp.float32) / math.sqrt(count_terms)
    factors = jnp.sum(jnp.where(matched[0], factor[None, :], 0.0), axis=1)
    counts = [c for c in (1, 2, held) if c <= held]
    choice = sum((most > c).astype(jnp.int32) for c in counts[:-1])
    sizes = [len(load_choices(homes, c)) for c in counts]
    firsts = [sum(sizes[:i]) for i in range(len(counts))]
    _, table = constants(homes)
    result = lax.switch(
        choice,
        [partial(listed_branch, c, first) for c, first in zip(counts, firsts)],
        jnp.asarray(table),
        voltages,
        history,
        block_pairs,
        listed,
        rank,
        source.reshape(-1).astype(jnp.int32),
        factors,
    )
    rows = ABLK * feed_count
    return result.reshape(1, capacity, 1, rows, rows)


def dense(voltages, history, block_pairs):
    antennas, feed_count, samples = voltages.shape
    spectra_dev = samples // NF
    frames = voltages.reshape(antennas, feed_count, spectra_dev, NF)
    tail_frames = frames[:, :, spectra_dev - (TAPS - 1) :, :]
    carried = from_behind(tail_frames, "pol", 1)
    stored = history.reshape(antennas, feed_count, TAPS - 1, NF)
    prior_frames = jnp.where(lax.axis_index("pol") == 0, stored, carried)
    signal = jnp.concatenate([prior_frames, frames], axis=2)
    window = prototype().reshape(TAPS, NF)
    filtered = jnp.zeros((antennas, feed_count, spectra_dev, NF), jnp.float32)
    for tap_index in range(TAPS):
        filtered = (
            filtered + window[tap_index] * signal[:, :, tap_index : tap_index + spectra_dev, :]
        )
    filtered = filtered.astype(jnp.bfloat16)
    n_chan = lax.axis_size("chan")
    n_blk = lax.axis_size("blk")
    turn_count = n_chan * n_blk
    dft_table = dft_rows()
    per_dev = dft_table.shape[2] // turn_count
    dft_table = dft_table.reshape(NF, 2, turn_count, per_dev)
    spectra = jnp.einsum(
        "afsn,nrdc->dafsrc", filtered, dft_table, preferred_element_type=jnp.float32
    ).astype(jnp.bfloat16)
    contract_len = spectra_dev * 2 * per_dev
    outgoing = spectra.reshape(turn_count, antennas, feed_count, contract_len)
    incoming = lax.all_to_all(outgoing, ("chan", "blk"), split_axis=0, concat_axis=0, tiled=True)
    block_rows = ABLK * feed_count
    block_count = block_pairs.shape[0]
    station = incoming.reshape(-1, block_rows, contract_len)
    left_rows = jnp.take(station, block_pairs[:, 0], axis=0)
    right_rows = jnp.take(station, block_pairs[:, 1], axis=0)
    right_split = right_rows.reshape(block_count, block_rows, spectra_dev, 2, per_dev)
    turned = jnp.stack([-right_split[:, :, :, 1, :], right_split[:, :, :, 0, :]], axis=3)
    turned = turned.reshape(block_count, block_rows, contract_len)
    partner = jnp.stack([right_rows, turned], axis=0)
    return jnp.einsum("bik,cbjk->cbij", left_rows, partner, preferred_element_type=jnp.float32)


def shards(voltages, history, block_pairs, owner_map, weights):
    antennas, feed_count, samples = voltages.shape
    spectra_dev = samples // NF
    if antennas % ABLK == 0 and lax.axis_size("blk") == 2 and lax.axis_size("pol") == 2:
        return listed_only(voltages, history, block_pairs, owner_map, weights)
    n_chan = lax.axis_size("chan")
    n_blk = lax.axis_size("blk")
    n_pol = lax.axis_size("pol")
    per_dev = NF // 2 // (n_chan * n_blk)
    block_rows = ABLK * feed_count
    block_count = block_pairs.shape[0]
    products = dense(voltages, history, block_pairs)
    count_terms = per_dev * n_blk * spectra_dev * n_pol
    factor = weights.astype(jnp.float32) / math.sqrt(count_terms)
    capacity = min(CAP, block_count - 1)
    parts_each = 2 // n_pol
    my_owner = jnp.reshape(lax.axis_index("blk"), (1,))
    mine_matched, mine_source, mine_filled = slot_sources(owner_map, my_owner, capacity)
    part_steps = jnp.arange(parts_each, dtype=jnp.int32)
    all_owners = jnp.arange(n_blk, dtype=jnp.int32)
    matched, source, filled = slot_sources(owner_map, all_owners, capacity)
    component = jnp.arange(n_pol, dtype=jnp.int32)[:, None] * parts_each + part_steps[None, :]
    take_index = component[None, :, None, :] * block_count + source[:, None, :, None]
    keep = jnp.broadcast_to(filled[:, None, :, None], take_index.shape).reshape(-1)
    flat_terms = products.reshape(2 * block_count, block_rows, block_rows)
    gathered = jnp.take(flat_terms, take_index.reshape(-1), axis=0)
    send_buffer = jnp.where(keep[:, None, None], gathered, 0.0)
    send_buffer = send_buffer.reshape(n_blk * n_pol, capacity * parts_each, block_rows, block_rows)
    received = lax.all_to_all(send_buffer, ("blk", "pol"), split_axis=0, concat_axis=0, tiled=True)
    summed = jnp.sum(received, axis=0)
    slot_scale = jnp.sum(jnp.where(mine_matched[0], factor[None, :], 0.0), axis=1)
    result = (
        summed.reshape(capacity, parts_each, block_rows, block_rows)
        * slot_scale[:, None, None, None]
    )
    return result.reshape(1, capacity, parts_each, block_rows, block_rows)


def solution(mesh):
    in_specs = (
        P(("group", "chan", "blk"), None, "pol"),
        P(("group", "chan", "blk"), None, None),
        P(),
        P(),
        P(),
    )
    out_specs = P(("group", "chan"), "blk", "pol", None, None)
    return jax.shard_map(shards, mesh=mesh, in_specs=in_specs, out_specs=out_specs, check_vma=False)
```

```python
import math
from functools import partial

import jax
import jax.numpy as jnp
import numpy as np
from jax import lax
from jax.experimental import pallas as pl
from jax.experimental.pallas import tpu as pltpu
from jax.sharding import PartitionSpec as P

ABLK = 64
NF = 2048
TAPS = 8
CAP = 4


def from_behind(block, axis, distance):
    devices = range(lax.axis_size(axis))
    route = [(i - distance, i) for i in devices if i - distance in devices]
    return lax.ppermute(block, axis, route)


def prototype():
    length = TAPS * NF
    position = jnp.arange(length, dtype=jnp.float32)
    taper_win = 0.54 - 0.46 * jnp.cos(2.0 * math.pi / (length - 1) * position)
    raw_taps = jnp.sinc((position - length / 2) / NF) * taper_win
    return raw_taps / jnp.sqrt(jnp.sum(raw_taps * raw_taps) / NF)


def dft_rows():
    sample = jnp.arange(NF, dtype=jnp.int32)[:, None]
    channel = jnp.arange(NF // 2, dtype=jnp.int32)[None, :]
    phases = (sample * channel % NF).astype(jnp.float32) * (2.0 * math.pi / NF)
    normalize = 1.0 / math.sqrt(NF)
    cosine = (jnp.cos(phases) * normalize).astype(jnp.bfloat16)
    sine_part = (jnp.sin(phases) * -normalize).astype(jnp.bfloat16)
    return jnp.stack([cosine, sine_part], axis=1)


def slot_sources(owner_map, owners, capacity):
    blocks = owner_map.shape[0]
    ordinal = jnp.arange(blocks, dtype=jnp.int32)
    same_owner = owner_map[None, :] == owner_map[:, None]
    earlier = ordinal[None, :] < ordinal[:, None]
    ranking = jnp.sum(jnp.logical_and(same_owner, earlier), axis=1)
    position = jnp.arange(capacity, dtype=jnp.int32)
    matched = jnp.logical_and(
        owner_map[None, None, :] == owners[:, None, None],
        ranking[None, None, :] == position[None, :, None],
    )
    source = jnp.sum(jnp.where(matched, ordinal[None, None, :], 0), axis=2)
    filled = jnp.any(matched, axis=2)
    return (matched, source, filled)


def constants(pieces):
    length = TAPS * NF
    position = np.arange(length, dtype=np.float64)
    taper_win = 0.54 - 0.46 * np.cos(2.0 * math.pi / (length - 1) * position)
    raw_taps = np.sinc((position - length / 2) / NF) * taper_win
    window = raw_taps / np.sqrt(np.sum(raw_taps * raw_taps) / NF)
    sample = np.arange(NF, dtype=np.int64)[:, None]
    channel = np.arange(NF // 2, dtype=np.int64)[None, :]
    phases = (sample * channel % NF).astype(np.float32) * np.float32(2.0 * math.pi / NF)
    phases = phases.astype(np.float64)
    normalize = np.float32(1.0 / math.sqrt(NF))
    cosine = np.cos(phases).astype(np.float32) * normalize
    sine = np.sin(phases).astype(np.float32) * -normalize
    table = np.stack([cosine, sine], axis=1).reshape(NF, 2, pieces, -1)
    table = table.transpose(0, 2, 1, 3).reshape(NF, -1)
    return window.astype(np.float32).reshape(TAPS, NF), table.astype(jnp.bfloat16)


def listed_blocks(block_pairs, homes, held):
    listed = jnp.any(
        block_pairs.reshape(-1)[:, None] == jnp.arange(homes * held, dtype=jnp.int32)[None, :],
        axis=0,
    ).reshape(homes, held)
    rank = jnp.cumsum(listed.astype(jnp.int32), axis=1) - 1
    most = jnp.max(rank[:, -1]) + 1
    return listed, rank, most


def select_kernel(local, source, target):
    target[...] = source[...].reshape(target.shape)


def select(source, local):
    _, feeds, samples = source.shape
    count = local.shape[0]
    step = 16
    chunks = ABLK // step
    return pl.pallas_call(
        select_kernel,
        grid_spec=pltpu.PrefetchScalarGridSpec(
            num_scalar_prefetch=1,
            grid=(count, chunks),
            in_specs=[
                pl.BlockSpec((step, feeds, samples), lambda k, c, local: (local[k] * chunks + c, 0, 0))
            ],
            out_specs=pl.BlockSpec((step * feeds, samples), lambda k, c, local: (k * chunks + c, 0)),
        ),
        out_shape=jax.ShapeDtypeStruct((count * ABLK * feeds, samples), source.dtype),
        compiler_params=pltpu.CompilerParams(vmem_limit_bytes=48 * 2**20),
        cost_estimate=pl.CostEstimate(
            flops=0, bytes_accessed=4 * count * ABLK * feeds * samples, transcendentals=0
        ),
    )(local, source)


def channelize_kernel(half, fresh, older, carried, window, table, spectra, filtered):
    rows, samples = fresh.shape
    count = samples // NF
    row_step, step = 16, 256

    @pl.when(pl.program_id(1) == 0)
    def _():
        first = half[0] == 0

        @pl.loop(0, rows // row_step)
        def _(r):
            at_rows = pl.ds(pl.multiple_of(r * row_step, row_step), row_step)

            @pl.loop(0, NF // step)
            def _(c):
                col = pl.multiple_of(c * step, step)
                taps = [window[pl.ds(t, 1), pl.ds(col, step)] for t in range(TAPS)]
                frames = []
                for i in range(TAPS - 1):
                    cols = pl.ds(col + i * NF, step)
                    was = older[at_rows, cols].astype(jnp.float32)
                    behind = pl.ds(col + (count - TAPS + 1 + i) * NF, step)
                    got = carried[at_rows, behind].astype(jnp.float32)
                    frames.append(jnp.where(first, was, got))
                for i in range(count):
                    cols = pl.ds(col + i * NF, step)
                    frames.append(fresh[at_rows, cols].astype(jnp.float32))
                for s in range(count):
                    total = taps[0] * frames[s]
                    for t in range(1, TAPS):
                        total = total + taps[t] * frames[s + t]
                    spot = pl.ds(pl.multiple_of(s * rows + r * row_step, row_step), row_step)
                    filtered[spot, pl.ds(col, step)] = total.astype(jnp.bfloat16)

    spectra[0, 0] = jnp.dot(
        filtered[...], table[...], preferred_element_type=jnp.float32
    ).astype(jnp.bfloat16)


def channelize(half, fresh, older, carried, window, table, count, homes):
    rows = fresh.shape[0] // count
    samples = fresh.shape[1]
    tall = rows * (samples // NF)
    per_dev = NF // homes
    past = older.shape[1]
    return pl.pallas_call(
        channelize_kernel,
        grid_spec=pltpu.PrefetchScalarGridSpec(
            num_scalar_prefetch=1,
            grid=(count, homes),
            in_specs=[
                pl.BlockSpec((rows, samples), lambda k, d, half: (k, 0)),
                pl.BlockSpec((rows, past), lambda k, d, half: (k, 0)),
                pl.BlockSpec((rows, samples), lambda k, d, half: (k, 0)),
                pl.BlockSpec((TAPS, NF), lambda k, d, half: (0, 0)),
                pl.BlockSpec((NF, per_dev), lambda k, d, half: (0, d)),
            ],
            out_specs=pl.BlockSpec((1, 1, tall, per_dev), lambda k, d, half: (d, k, 0, 0)),
            scratch_shapes=[pltpu.VMEM((tall, NF), jnp.bfloat16)],
        ),
        out_shape=jax.ShapeDtypeStruct((homes, count, tall, per_dev), jnp.bfloat16),
        compiler_params=pltpu.CompilerParams(vmem_limit_bytes=56 * 2**20),
        cost_estimate=pl.CostEstimate(
            flops=2 * count * tall * NF * NF,
            bytes_accessed=16 * 2**20 * count,
            transcendentals=0,
        ),
    )(half, fresh, older, carried, window, table)


def correlate_kernel(
    homes, n_blk, loads, blocks, capacity,
    places, factors, outgoing, result,
    station, products, summed, from_pol, to_blk, from_blk, send, receive, own,
):
    chan, blk, pol = (lax.axis_index(a) for a in ("chan", "blk", "pol"))
    me = chan * n_blk + blk
    rows = products.shape[-1]
    frames = outgoing.shape[2] // rows

    def member(other):
        return {"chan": other // n_blk, "blk": lax.rem(other, n_blk)}

    barrier = pltpu.get_barrier_semaphore()
    for step in range(1, homes):
        pl.semaphore_signal(
            barrier, inc=1, device_id=member(lax.rem(me + step, homes)),
            device_id_type=pl.DeviceIdType.MESH,
        )
    pl.semaphore_signal(
        barrier, inc=1, device_id={"pol": 1 - pol}, device_id_type=pl.DeviceIdType.MESH
    )
    pl.semaphore_wait(barrier, homes)

    def loaded(device, slot):
        full = [d for d in range(homes) if loads[d] > slot]
        if len(full) == homes:
            return None
        yes = device == full[0]
        for d in full[1:]:
            yes = jnp.logical_or(yes, device == d)
        return yes

    def when(yes, action):
        if yes is None:
            action()
        else:
            pl.when(yes)(action)

    copies = []
    count = max(loads)
    steps = (4, 3, 5, 2, 6, 1, 7) if homes == 8 else tuple(range(1, homes))
    for slot in range(count):
        sending = loaded(me, slot)
        for index, step in enumerate(steps):
            other = lax.rem(me + step, homes)
            copy = pltpu.make_async_remote_copy(
                src_ref=outgoing.at[other, slot],
                dst_ref=station.at[me, slot],
                send_sem=send.at[slot * homes + index],
                recv_sem=receive.at[slot * homes + index],
                device_id=member(other),
                device_id_type=pl.DeviceIdType.MESH,
            )
            when(sending, copy.start)
            coming = loaded(lax.rem(me - step + homes, homes), slot)
            copies.append((copy, sending, coming))
    mine = pltpu.make_async_copy(outgoing.at[me], station.at[me], own)
    mine.start()
    mine.wait()
    for copy, sending, coming in copies:
        when(sending, copy.wait_send)
        when(coming, copy.wait_recv)

    half = station.shape[-1] // 2
    over = (((1,), (1,)), ((), ()))
    for b in range(blocks):
        left_home, left_at = places[b], places[blocks + b]
        right_home, right_at = places[2 * blocks + b], places[3 * blocks + b]
        real = jnp.zeros((rows, rows), jnp.float32)
        imag = jnp.zeros((rows, rows), jnp.float32)
        for s in range(frames):
            span = pl.ds(s * rows, rows)
            left = station[left_home, left_at, span, :]
            right = station[right_home, right_at, span, :]
            turned = jnp.concatenate([-right[:, half:], right[:, :half]], axis=1)
            real += lax.dot_general(left, right, over, preferred_element_type=jnp.float32)
            imag += lax.dot_general(left, turned, over, preferred_element_type=jnp.float32)
        products[0, b] = real
        products[1, b] = imag

    last = count * homes
    swap = pltpu.make_async_remote_copy(
        src_ref=products.at[1 - pol],
        dst_ref=from_pol,
        send_sem=send.at[last],
        recv_sem=receive.at[last],
        device_id={"pol": 1 - pol},
        device_id_type=pl.DeviceIdType.MESH,
    )
    swap.start()
    swap.wait()
    summed[...] = products[pol] + from_pol[...]
    for c in range(capacity):
        to_blk[c] = summed[places[4 * blocks + capacity + c]]
    swap = pltpu.make_async_remote_copy(
        src_ref=to_blk,
        dst_ref=from_blk,
        send_sem=send.at[last + 1],
        recv_sem=receive.at[last + 1],
        device_id={"blk": 1 - blk},
        device_id_type=pl.DeviceIdType.MESH,
    )
    swap.start()
    swap.wait()
    for c in range(capacity):
        result[c] = (summed[places[4 * blocks + c]] + from_blk[c]) * factors[c]


def correlate(loads, serial, blocks, n_blk, places, factors, outgoing):
    homes, count, tall, per_dev = outgoing.shape
    capacity = factors.shape[0]
    rows = 2 * ABLK
    square = lambda *lead: pltpu.VMEM((*lead, rows, rows), jnp.float32)
    return pl.pallas_call(
        partial(correlate_kernel, homes, n_blk, loads, blocks, capacity),
        out_shape=jax.ShapeDtypeStruct((capacity, rows, rows), jnp.float32),
        in_specs=[
            pl.BlockSpec(memory_space=pltpu.SMEM),
            pl.BlockSpec(memory_space=pltpu.SMEM),
            pl.BlockSpec(memory_space=pl.ANY),
        ],
        out_specs=pl.BlockSpec(memory_space=pltpu.VMEM),
        scratch_shapes=[
            pltpu.VMEM(outgoing.shape, jnp.bfloat16),
            square(2, blocks),
            square(blocks),
            square(blocks),
            square(capacity),
            square(capacity),
            pltpu.SemaphoreType.DMA((count * homes + 2,)),
            pltpu.SemaphoreType.DMA((count * homes + 2,)),
            pltpu.SemaphoreType.DMA,
        ],
        compiler_params=pltpu.CompilerParams(
            collective_id=serial, has_side_effects=True, vmem_limit_bytes=48 * 2**20
        ),
    )(places, factors, outgoing)


def load_choices(homes, count):
    lighter = []
    if count == 2:
        lighter = [tuple(2 if d == e else 1 for d in range(homes)) for e in range(homes)]
    return lighter + [(count,) * homes]


def listed_branch(count, serial, table, voltages, history, block_pairs, listed, rank, sources, factors):
    homes = lax.axis_size("chan") * lax.axis_size("blk")
    held = voltages.shape[0] // ABLK
    window, _ = constants(homes)
    me = lax.axis_index("chan") * lax.axis_size("blk") + lax.axis_index("blk")
    mine = lax.dynamic_index_in_dim(jnp.where(listed, rank, -1), me, 0, keepdims=False)
    order = jnp.arange(count, dtype=jnp.int32)
    local = jnp.sum(
        jnp.where(mine[None, :] == order[:, None], jnp.arange(held, dtype=jnp.int32)[None, :], 0),
        axis=1,
    ).astype(jnp.int32)
    fresh = select(voltages, local)
    carried = from_behind(fresh, "pol", 1)
    older = select(history, local)
    half = lax.axis_index("pol").astype(jnp.int32).reshape(1)
    outgoing = channelize(half, fresh, older, carried, jnp.asarray(window), table, count, homes)
    pairs = block_pairs.T.astype(jnp.int32)
    home = pairs // held
    at = jnp.take(rank.reshape(-1), pairs)
    places = jnp.concatenate([home[0], at[0], home[1], at[1], sources]).astype(jnp.int32)
    choices = load_choices(homes, count)
    has = rank[:, -1] + 1
    fits = jnp.all(has[None, :] <= jnp.array(choices, jnp.int32), axis=1)
    ordinal = jnp.arange(len(choices), dtype=jnp.int32)
    return lax.switch(
        jnp.min(jnp.where(fits, ordinal, len(choices) - 1)),
        [
            partial(correlate, c, serial + i, block_pairs.shape[0], lax.axis_size("blk"))
            for i, c in enumerate(choices)
        ],
        places,
        factors,
        outgoing,
    )


def listed_only(voltages, history, block_pairs, owner_map, weights):
    antennas, feed_count, samples = voltages.shape
    n_chan, n_blk, n_pol = (lax.axis_size(a) for a in ("chan", "blk", "pol"))
    homes = n_chan * n_blk
    held = antennas // ABLK
    blocks = block_pairs.shape[0]
    blk = lax.axis_index("blk")
    listed, rank, most = listed_blocks(block_pairs, homes, held)
    capacity = min(CAP, blocks - 1)
    owners = jnp.stack([blk, 1 - blk]).astype(jnp.int32)
    matched, source, filled = slot_sources(owner_map, owners, capacity)
    count_terms = NF // 2 // n_chan * (samples // NF) * n_pol
    factor = weights.astype(jnp.float32) / math.sqrt(count_terms)
    factors = jnp.sum(jnp.where(matched[0], factor[None, :], 0.0), axis=1)
    counts = [c for c in (1, 2, held) if c <= held]
    choice = sum((most > c).astype(jnp.int32) for c in counts[:-1])
    sizes = [len(load_choices(homes, c)) for c in counts]
    firsts = [sum(sizes[:i]) for i in range(len(counts))]
    _, table = constants(homes)
    result = lax.switch(
        choice,
        [partial(listed_branch, c, first) for c, first in zip(counts, firsts)],
        jnp.asarray(table),
        voltages,
        history,
        block_pairs,
        listed,
        rank,
        source.reshape(-1).astype(jnp.int32),
        factors,
    )
    rows = ABLK * feed_count
    return result.reshape(1, capacity, 1, rows, rows)


def dense(voltages, history, block_pairs):
    antennas, feed_count, samples = voltages.shape
    spectra_dev = samples // NF
    frames = voltages.reshape(antennas, feed_count, spectra_dev, NF)
    tail_frames = frames[:, :, spectra_dev - (TAPS - 1) :, :]
    carried = from_behind(tail_frames, "pol", 1)
    stored = history.reshape(antennas, feed_count, TAPS - 1, NF)
    prior_frames = jnp.where(lax.axis_index("pol") == 0, stored, carried)
    signal = jnp.concatenate([prior_frames, frames], axis=2)
    window = prototype().reshape(TAPS, NF)
    filtered = jnp.zeros((antennas, feed_count, spectra_dev, NF), jnp.float32)
    for tap_index in range(TAPS):
        filtered = (
            filtered + window[tap_index] * signal[:, :, tap_index : tap_index + spectra_dev, :]
        )
    filtered = filtered.astype(jnp.bfloat16)
    n_chan = lax.axis_size("chan")
    n_blk = lax.axis_size("blk")
    turn_count = n_chan * n_blk
    dft_table = dft_rows()
    per_dev = dft_table.shape[2] // turn_count
    dft_table = dft_table.reshape(NF, 2, turn_count, per_dev)
    spectra = jnp.einsum(
        "afsn,nrdc->dafsrc", filtered, dft_table, preferred_element_type=jnp.float32
    ).astype(jnp.bfloat16)
    contract_len = spectra_dev * 2 * per_dev
    outgoing = spectra.reshape(turn_count, antennas, feed_count, contract_len)
    incoming = lax.all_to_all(outgoing, ("chan", "blk"), split_axis=0, concat_axis=0, tiled=True)
    block_rows = ABLK * feed_count
    block_count = block_pairs.shape[0]
    station = incoming.reshape(-1, block_rows, contract_len)
    left_rows = jnp.take(station, block_pairs[:, 0], axis=0)
    right_rows = jnp.take(station, block_pairs[:, 1], axis=0)
    right_split = right_rows.reshape(block_count, block_rows, spectra_dev, 2, per_dev)
    turned = jnp.stack([-right_split[:, :, :, 1, :], right_split[:, :, :, 0, :]], axis=3)
    turned = turned.reshape(block_count, block_rows, contract_len)
    partner = jnp.stack([right_rows, turned], axis=0)
    return jnp.einsum("bik,cbjk->cbij", left_rows, partner, preferred_element_type=jnp.float32)


def shards(voltages, history, block_pairs, owner_map, weights):
    antennas, feed_count, samples = voltages.shape
    spectra_dev = samples // NF
    if antennas % ABLK == 0 and lax.axis_size("blk") == 2 and lax.axis_size("pol") == 2:
        return listed_only(voltages, history, block_pairs, owner_map, weights)
    n_chan = lax.axis_size("chan")
    n_blk = lax.axis_size("blk")
    n_pol = lax.axis_size("pol")
    per_dev = NF // 2 // (n_chan * n_blk)
    block_rows = ABLK * feed_count
    block_count = block_pairs.shape[0]
    products = dense(voltages, history, block_pairs)
    count_terms = per_dev * n_blk * spectra_dev * n_pol
    factor = weights.astype(jnp.float32) / math.sqrt(count_terms)
    capacity = min(CAP, block_count - 1)
    parts_each = 2 // n_pol
    my_owner = jnp.reshape(lax.axis_index("blk"), (1,))
    mine_matched, mine_source, mine_filled = slot_sources(owner_map, my_owner, capacity)
    part_steps = jnp.arange(parts_each, dtype=jnp.int32)
    all_owners = jnp.arange(n_blk, dtype=jnp.int32)
    matched, source, filled = slot_sources(owner_map, all_owners, capacity)
    component = jnp.arange(n_pol, dtype=jnp.int32)[:, None] * parts_each + part_steps[None, :]
    take_index = component[None, :, None, :] * block_count + source[:, None, :, None]
    keep = jnp.broadcast_to(filled[:, None, :, None], take_index.shape).reshape(-1)
    flat_terms = products.reshape(2 * block_count, block_rows, block_rows)
    gathered = jnp.take(flat_terms, take_index.reshape(-1), axis=0)
    send_buffer = jnp.where(keep[:, None, None], gathered, 0.0)
    send_buffer = send_buffer.reshape(n_blk * n_pol, capacity * parts_each, block_rows, block_rows)
    received = lax.all_to_all(send_buffer, ("blk", "pol"), split_axis=0, concat_axis=0, tiled=True)
    summed = jnp.sum(received, axis=0)
    slot_scale = jnp.sum(jnp.where(mine_matched[0], factor[None, :], 0.0), axis=1)
    result = (
        summed.reshape(capacity, parts_each, block_rows, block_rows)
        * slot_scale[:, None, None, None]
    )
    return result.reshape(1, capacity, parts_each, block_rows, block_rows)


def solution(mesh):
    in_specs = (
        P(("group", "chan", "blk"), None, "pol"),
        P(("group", "chan", "blk"), None, None),
        P(),
        P(),
        P(),
    )
    out_specs = P(("group", "chan"), "blk", "pol", None, None)
    return jax.shard_map(shards, mesh=mesh, in_specs=in_specs, out_specs=out_specs, check_vma=False)
```
